32 devices in a mesh: lat: 4 (over y, x), lon: 4 (over z), feat: 2 (over core).
Axes of the slice: x: 2, y: 2, z: 4, core: 2. Of those that a mesh axis runs over, the one named last changes fastest.
Arguments:
- atmosphere: float32 [384, 768, 256], P('lat', 'lon', 'feat'), may hold values from -6 to 6
- spectral_weight: float32 [2, 384, 256, 256], P(None, ('lat', 'lon'), None, 'feat'), may hold values from -0.25 to 0.25
- mlp_in: float32 [256, 768], P(None, 'feat'), may hold values from -0.375 to 0.375
- mlp_out: float32 [768, 256], P(None, 'feat'), may hold values from -0.21875 to 0.21875
- ocean_state: float32 [256, 64, 256], P('lat', 'lon', 'feat'), may hold values from -6 to 6
- depth_kernel: float32 [7, 7, 256], P(None, None, 'feat'), may hold values from -0.875 to 0.875
- depth_bias: float32 [256], P('feat'), may hold values from -4 to 4
- norm_gain: float32 [256], replicated, may hold values from 0.5 to 1.5
- ocean_up: float32 [256, 1024], P(None, 'feat'), may hold values from -0.375 to 0.375
- ocean_down: float32 [1024, 256], P(None, 'feat'), may hold values from -0.1875 to 0.1875
- ocean_bias: float32 [256], P('feat'), may hold values from -3 to 3
- layer_scale: float32 [256], P('feat'), may hold values from 0.5 to 1.5
- flux_weight: float32 [256, 256], P(None, 'feat'), may hold values from -0.375 to 0.375
- regrid_rows: int32 [4, 4, 4, 256], P('lat', 'lon'), may hold values from 0 to 18431
- ocean_rows: int32 [256, 64], P('lat', 'lon'), may hold values from 0 to 1023
- land_mask: int32 [32, 8], P('lat', 'lon'), may hold values 0 or 1
Outputs:
- atmos_next: float32 [384, 768, 256], P('lat', 'lon', 'feat')
- ocean_next: float32 [256, 64, 256], P('lat', 'lon', 'feat')
The draws below stay inside these ranges and needn't reach their ends.
Inputs may be any that keep to these rules, and one draw needn't show every extreme that they name: regrid_rows[a, s, b, k] counts the points of latitude band a and longitude sector s latitude-major, 192 to a latitude. ocean_rows[i, o] = s * 256 + k names the k-th point that the cell's tile takes from sector s. `land_mask`: 1 for a sea block, 0 for a land block.
All inputs are finite; a program needn't handle non-finite values.
Results may differ from the reference program's by a relative error of at most 0.0003.
Values sent between devices are 32-bit elements; how exact they have to be, the bound alone decides.
A program may use at most 192 MiB of HBM per device.

```python
import math
import jax
import jax.numpy as jnp
from jax import lax

C = 256
HID = 768
NLAT = 384
NLON = 768
LMAX = 384
MMAX = 256
CO = 256
HO = 1024
KERNEL = 7
BLOCK = 8
OLAT = 256
OLON = 64
PICKS = 256
ATM_ROWS = 18432
N_LAT = 4
N_LON = 4


def set_ends(values, rng, least, largest):
    dims = values.shape
    spot = [jax.random.randint(jax.random.fold_in(rng, axis), (), 0, dims[axis]) for axis in range(len(dims))]
    values = values.at[tuple(spot)].set(least)
    longest = dims.index(max(dims))
    spot[longest] = (spot[longest] + 1) % dims[longest]
    return values.at[tuple(spot)].set(largest)


def levels(stream_key, extent, shards, low, high):
    def one(axis_at, blocks):
        draws = jax.random.uniform(jax.random.fold_in(jax.random.fold_in(stream_key, 6), axis_at), (blocks,), jnp.float32, low / len(shards), high / len(shards))
        return jnp.repeat(jnp.exp(draws), extent[axis_at] // blocks).reshape((-1,) + (1,) * (len(extent) - axis_at - 1))

    loudness = one(*shards[0])
    for cut in shards[1:]:
        loudness = loudness * one(*cut)
    return loudness


def gaussian(own_key, extent, spread, reach, split=(), kind=jnp.bfloat16):
    array = spread * jax.random.normal(own_key, extent, jnp.float32)
    if split:
        array = array * levels(own_key, extent, split, -0.22, 0.18)
    return jnp.clip(array, -reach, reach).astype(kind)


def setup_inputs(seed: int = 0) -> dict:
    arg_keys = jax.random.split(jax.random.key(seed), 17)
    return {
        "atmosphere": gaussian(arg_keys[0], (NLAT, NLON, C), 1.0, 6.0, ((0, 4), (1, 4), (2, 2)), jnp.float32),
        "spectral_weight": gaussian(arg_keys[1], (2, LMAX, C, C), (2 * C) ** -0.5, 0.25, ((1, 16), (3, 2)), jnp.float32),
        "mlp_in": gaussian(arg_keys[2], (C, HID), C ** -0.5, 0.375, ((1, 2),), jnp.float32),
        "mlp_out": gaussian(arg_keys[3], (HID, C), HID ** -0.5, 0.21875, ((1, 2),), jnp.float32),
        "ocean_state": gaussian(arg_keys[4], (OLAT, OLON, CO), 1.0, 6.0, ((0, 4), (1, 4), (2, 2)), jnp.float32),
        "depth_kernel": gaussian(arg_keys[5], (KERNEL, KERNEL, CO), (KERNEL * KERNEL) ** -0.5, 0.875, ((2, 2),), jnp.float32),
        "depth_bias": gaussian(arg_keys[6], (CO,), 0.7, 4.0, ((0, 2),), jnp.float32),
        "norm_gain": jnp.clip(jax.random.uniform(arg_keys[7], (CO,), jnp.float32, 0.5, 1.5), 0.5, 1.5),
        "ocean_up": gaussian(arg_keys[8], (CO, HO), CO ** -0.5, 0.375, ((1, 2),), jnp.float32),
        "ocean_down": gaussian(arg_keys[9], (HO, CO), HO ** -0.5, 0.1875, ((1, 2),), jnp.float32),
        "ocean_bias": gaussian(arg_keys[10], (CO,), 0.5, 3.0, ((0, 2),), jnp.float32),
        "layer_scale": jnp.clip(0.5 + 1.0 * jax.random.uniform(arg_keys[11], (CO,), jnp.float32) ** levels(arg_keys[11], (CO,), ((0, 2),), -0.2, 0.2), 0.5, 1.5),
        "flux_weight": gaussian(arg_keys[12], (C, CO), C ** -0.5, 0.375, ((1, 2),), jnp.float32),
        "regrid_rows": set_ends(jax.random.randint(arg_keys[13], (N_LAT, N_LON, N_LON, PICKS), 0, ATM_ROWS), jax.random.fold_in(arg_keys[13], 1), 0, ATM_ROWS - 1).astype(jnp.int32),
        "ocean_rows": set_ends(jax.random.randint(arg_keys[14], (OLAT, OLON), 0, N_LON * PICKS), jax.random.fold_in(arg_keys[14], 1), 0, (N_LON * PICKS) - 1).astype(jnp.int32),
        "land_mask": set_ends((jax.random.randint(arg_keys[15], (OLAT // BLOCK, OLON // BLOCK), 0, 4) < 3).astype(jnp.int32), jax.random.fold_in(arg_keys[15], 1), 0, 1),
    }


best_precision = lax.Precision.HIGHEST

def legendre_table(orders, degree_count, lat_count, order_limit):
    index_lat = jnp.arange(lat_count, dtype=jnp.int32).astype(jnp.float32)
    colat = math.pi * (index_lat + 0.5) / lat_count
    cosine = jnp.cos(colat)
    sine = jnp.sin(colat)
    order_f = orders.astype(jnp.float32)[:, None]
    steps_k = jnp.arange(1, order_limit + 1, dtype=jnp.int32)
    step_f = steps_k.astype(jnp.float32)
    log_terms = jnp.log((2.0 * step_f + 1.0) / (2.0 * step_f))
    log_norm = lax.optimization_barrier(jnp.sum(jnp.where(steps_k[None, :] <= orders[:, None], log_terms[None, :], 0.0), axis=1))
    log_start = 0.5 * (math.log(0.5) + log_norm[:, None]) + order_f * jnp.log(sine)[None, :]
    zeros_grid = jnp.zeros((orders.shape[0], lat_count), jnp.float32)

    def advance(carry, degree):
        current, previous, shift = carry
        deg_f = degree.astype(jnp.float32)
        order_sq = order_f * order_f
        factor_a = jnp.sqrt(jnp.maximum(4.0 * deg_f * deg_f - 1.0, 0.0) / jnp.maximum(deg_f * deg_f - order_sq, 1.0))
        below = deg_f - 1.0
        factor_b = jnp.sqrt(jnp.maximum(below * below - order_sq, 0.0) / jnp.maximum(4.0 * below * below - 1.0, 1.0))
        recurred = factor_a * (cosine[None, :] * current - factor_b * previous)
        fresh = jnp.where(degree == orders[:, None], 1.0, jnp.where(degree > orders[:, None], recurred, 0.0))
        large = jnp.abs(fresh) > 2.0 ** 32
        rescale = jnp.where(large, 2.0 ** (-32), 1.0)
        fresh = fresh * rescale
        shift = shift + jnp.where(large, 32.0, 0.0)
        value = fresh * jnp.exp(log_start + shift * math.log(2.0))
        return ((fresh, current * rescale, shift), value)
    final_state, table = lax.scan(advance, (zeros_grid, zeros_grid, zeros_grid), jnp.arange(degree_count, dtype=jnp.int32), unroll=16)
    return table

def quadrature(lat_ids, lat_count):
    colat = math.pi * (lat_ids.astype(jnp.float32) + 0.5) / lat_count
    return jnp.sin(colat) * (math.pi / lat_count)

def forward_table(lon_count, order_count):
    lon_ids = jnp.arange(lon_count, dtype=jnp.int32)[:, None]
    order_ids = jnp.arange(order_count, dtype=jnp.int32)[None, :]
    phase = 2.0 * math.pi / lon_count * (lon_ids * order_ids % lon_count).astype(jnp.float32)
    return jnp.stack([jnp.cos(phase), -jnp.sin(phase)], axis=0) / lon_count

def inverse_table(lon_count, order_count):
    order_ids = jnp.arange(order_count, dtype=jnp.int32)[:, None]
    lon_ids = jnp.arange(lon_count, dtype=jnp.int32)[None, :]
    phase = 2.0 * math.pi / lon_count * (order_ids * lon_ids % lon_count).astype(jnp.float32)
    weight = jnp.where(order_ids == 0, 1.0, 2.0)
    return jnp.stack([jnp.cos(phase) * weight, -jnp.sin(phase) * weight], axis=0)

def reference(atmosphere, spectral_weight, mlp_in, mlp_out, ocean_state, depth_kernel, depth_bias, norm_gain, ocean_up, ocean_down, ocean_bias, layer_scale, flux_weight, regrid_rows, ocean_rows, land_mask):
    lat_ids = jnp.arange(NLAT, dtype=jnp.int32)
    table = legendre_table(jnp.arange(MMAX, dtype=jnp.int32), LMAX, NLAT, MMAX)
    quad = quadrature(lat_ids, NLAT)
    modes = jnp.einsum('jnc,rnm->mrjc', atmosphere, forward_table(NLON, MMAX), precision=best_precision)
    coeffs = jnp.einsum('lmj,mrjc->lrmc', table * quad[None, None, :], modes, precision=best_precision)
    real_part = jnp.einsum('lmc,lcd->lmd', coeffs[:, 0], spectral_weight[0], precision=best_precision) - jnp.einsum('lmc,lcd->lmd', coeffs[:, 1], spectral_weight[1], precision=best_precision)
    imag_part = jnp.einsum('lmc,lcd->lmd', coeffs[:, 1], spectral_weight[0], precision=best_precision) + jnp.einsum('lmc,lcd->lmd', coeffs[:, 0], spectral_weight[1], precision=best_precision)
    mixed = jnp.stack([real_part, imag_part], axis=1)
    grid_modes = jnp.einsum('lmj,lrmc->jrmc', table, mixed, precision=best_precision)
    spectral_field = jnp.einsum('jrmc,rmn->jnc', grid_modes, inverse_table(NLON, MMAX), precision=best_precision)
    summed = atmosphere + spectral_field

    def row_block(rows):
        hidden = jax.nn.gelu(jnp.dot(rows, mlp_in, precision=best_precision, preferred_element_type=jnp.float32), approximate=False)
        return rows + jnp.dot(hidden, mlp_out, precision=best_precision, preferred_element_type=jnp.float32)
    atmos_next = lax.map(row_block, summed)
    row_ids = jnp.arange(OLAT, dtype=jnp.int32)[:, None]
    col_ids = jnp.arange(OLON, dtype=jnp.int32)[None, :]
    band = jnp.broadcast_to(row_ids // (OLAT // N_LAT), (OLAT, OLON))
    tile = jnp.broadcast_to(col_ids // (OLON // N_LON), (OLAT, OLON))
    sector = ocean_rows // PICKS
    slot_ids = ocean_rows % PICKS
    local_ids = regrid_rows[band, sector, tile, slot_ids]
    atm_lat = NLAT // N_LAT
    atm_lon = NLON // N_LON
    lat_pick = band * atm_lat + local_ids // atm_lon
    lon_pick = sector * atm_lon + local_ids % atm_lon
    picked = atmosphere[lat_pick, lon_pick]
    forcing = jnp.dot(picked.reshape(-1, C), flux_weight, precision=best_precision, preferred_element_type=jnp.float32).reshape(OLAT, OLON, CO)
    half_side = KERNEL // 2
    padded = jnp.pad(ocean_state, ((half_side, half_side), (half_side, half_side), (0, 0)))
    conv = jnp.zeros((OLAT, OLON, CO), jnp.float32) + depth_bias
    for tap_row in range(KERNEL):
        for tap_col in range(KERNEL):
            conv = conv + padded[tap_row:tap_row + OLAT, tap_col:tap_col + OLON] * depth_kernel[tap_row, tap_col]
    joined = conv + forcing
    row_mean = lax.optimization_barrier(jnp.mean(joined, axis=-1, keepdims=True))
    centered = joined - row_mean
    variance = lax.optimization_barrier(jnp.mean(centered * centered, axis=-1, keepdims=True))
    normed = centered * lax.rsqrt(variance + 1e-06) * norm_gain
    ocean_hidden = jax.nn.gelu(jnp.dot(normed.reshape(-1, CO), ocean_up, precision=best_precision, preferred_element_type=jnp.float32), approximate=False)
    update = (jnp.dot(ocean_hidden, ocean_down, precision=best_precision, preferred_element_type=jnp.float32) + ocean_bias).reshape(OLAT, OLON, CO)
    cell_mask = jnp.broadcast_to(land_mask[:, None, :, None], (OLAT // BLOCK, BLOCK, OLON // BLOCK, BLOCK)).reshape(OLAT, OLON).astype(jnp.float32)
    ocean_next = ocean_state + cell_mask[:, :, None] * layer_scale * update
    return (atmos_next, ocean_next)
```

```python
import math

import jax
import jax.numpy as jnp
from jax import lax
from jax.experimental import pallas as pl
from jax.experimental.pallas import tpu as pltpu
from jax.sharding import PartitionSpec as P

C = 256
NLAT = 384
NLON = 768
LMAX = 384
MMAX = 256
KERNEL = 7
BLOCK = 8


best_precision = lax.Precision.HIGH


def with_halo(block, sides, width):
    for axis, dim in sides:
        count = lax.axis_size(axis)
        forward = [(i, i + 1) for i in range(count - 1)]
        backward = [(target, source) for source, target in forward]
        low = lax.ppermute(
            lax.slice_in_dim(block, block.shape[dim] - width, None, axis=dim), axis, forward
        )
        high = lax.ppermute(lax.slice_in_dim(block, 0, width, axis=dim), axis, backward)
        block = jnp.concatenate([low, block, high], axis=dim)
    return block


def legendre_table(orders, degree_count, lat_count, order_limit):
    index_lat = jnp.arange(lat_count, dtype=jnp.int32).astype(jnp.float32)
    colat = math.pi * (index_lat + 0.5) / lat_count
    cosine = jnp.cos(colat)
    sine = jnp.sin(colat)
    order_f = orders.astype(jnp.float32)[:, None]
    steps_k = jnp.arange(1, order_limit + 1, dtype=jnp.int32)
    step_f = steps_k.astype(jnp.float32)
    log_terms = jnp.log((2.0 * step_f + 1.0) / (2.0 * step_f))
    log_norm = jnp.sum(
        jnp.where(steps_k[None, :] <= orders[:, None], log_terms[None, :], 0.0), axis=1
    )
    log_start = 0.5 * (math.log(0.5) + log_norm[:, None]) + order_f * jnp.log(sine)[None, :]
    degree_f = jnp.arange(degree_count, dtype=jnp.int32).astype(jnp.float32)[:, None, None]
    order_sq = order_f * order_f
    factor_a = jnp.sqrt(
        jnp.maximum(4.0 * degree_f * degree_f - 1.0, 0.0)
        / jnp.maximum(degree_f * degree_f - order_sq, 1.0)
    )
    below = degree_f - 1.0
    factor_b = jnp.sqrt(
        jnp.maximum(below * below - order_sq, 0.0) / jnp.maximum(4.0 * below * below - 1.0, 1.0)
    )
    count = orders.shape[0]
    order_grid = jnp.broadcast_to(orders[:, None], (count, lat_count))
    chunk = math.gcd(degree_count, 48)

    def recur(start_ref, order_ref, cosine_ref, a_ref, b_ref, table_ref, state):
        @pl.when(pl.program_id(0) == 0)
        def _():
            state[...] = jnp.zeros_like(state)

        log_scale = start_ref[...]
        order = order_ref[...]
        cos_grid = cosine_ref[...]
        first = pl.program_id(0) * chunk
        current, previous, shift = state[0], state[1], state[2]
        for step in range(chunk):
            degree = first + step
            recurred = a_ref[step] * (cos_grid * current - b_ref[step] * previous)
            fresh = jnp.where(
                degree == order, 1.0, jnp.where(degree > order, recurred, 0.0)
            )
            large = jnp.abs(fresh) > 2.0**32
            rescale = jnp.where(large, 2.0 ** (-32), 1.0)
            fresh = fresh * rescale
            shift = shift + jnp.where(large, 32.0, 0.0)
            table_ref[step] = fresh * jnp.exp(log_scale + shift * math.log(2.0))
            current, previous = fresh, current * rescale
        state[0], state[1], state[2] = current, previous, shift

    whole = pl.BlockSpec((count, lat_count), lambda i: (0, 0))
    factor = pl.BlockSpec((chunk, count, 1), lambda i: (i, 0, 0))
    return pl.pallas_call(
        recur,
        grid=(degree_count // chunk,),
        in_specs=[whole, whole, whole, factor, factor],
        out_specs=pl.BlockSpec((chunk, count, lat_count), lambda i: (i, 0, 0)),
        out_shape=jax.ShapeDtypeStruct((degree_count, count, lat_count), jnp.float32),
        scratch_shapes=[pltpu.VMEM((3, count, lat_count), jnp.float32)],
        compiler_params=pltpu.CompilerParams(vmem_limit_bytes=32 * 2**20),
        cost_estimate=pl.CostEstimate(
            flops=60 * degree_count * count * lat_count,
            bytes_accessed=60 * degree_count * count * lat_count,
            transcendentals=degree_count * count * lat_count,
        ),
    )(
        log_start,
        order_grid,
        jnp.broadcast_to(cosine[None, :], (count, lat_count)),
        factor_a,
        factor_b,
    )


def quadrature(lat_ids, lat_count):
    colat = math.pi * (lat_ids.astype(jnp.float32) + 0.5) / lat_count
    return jnp.sin(colat) * (math.pi / lat_count)


def forward_table(lon_count, order_count):
    lon_ids = jnp.arange(lon_count, dtype=jnp.int32)[:, None]
    order_ids = jnp.arange(order_count, dtype=jnp.int32)[None, :]
    phase = 2.0 * math.pi / lon_count * (lon_ids * order_ids % lon_count).astype(jnp.float32)
    return jnp.stack([jnp.cos(phase), -jnp.sin(phase)], axis=0) / lon_count


def inverse_table(lon_count, order_count):
    order_ids = jnp.arange(order_count, dtype=jnp.int32)[:, None]
    lon_ids = jnp.arange(lon_count, dtype=jnp.int32)[None, :]
    phase = 2.0 * math.pi / lon_count * (order_ids * lon_ids % lon_count).astype(jnp.float32)
    weight = jnp.where(order_ids == 0, 1.0, 2.0)
    return jnp.stack([jnp.cos(phase) * weight, -jnp.sin(phase) * weight], axis=0)


def regroup(blocks):
    return lax.all_to_all(blocks, "lon", split_axis=0, concat_axis=2, tiled=True)[0]


def split_value(value):
    high = value.astype(jnp.bfloat16)
    return high, (value - high.astype(jnp.float32)).astype(jnp.bfloat16)


def split_dot(left, right_high, right_low):
    left_high, left_low = split_value(left)

    def part(one, other):
        return jnp.dot(one, other, preferred_element_type=jnp.float32)

    return part(left_high, right_high) + (
        part(left_high, right_low) + part(left_low, right_high)
    )


def mlp_kernel(rows_ref, up_ref, down_ref, out_ref, up_high, up_low, down_high, down_low):
    @pl.when(pl.program_id(0) == 0)
    def _():
        up_high[...], up_low[...] = split_value(up_ref[...])
        down_high[...], down_low[...] = split_value(down_ref[...])

    rows = rows_ref[...]
    pre = split_dot(rows, up_high[...], up_low[...])
    hidden = 0.5 * pre * (1.0 + lax.erf(pre * math.sqrt(0.5)))
    out_ref[...] = rows + split_dot(hidden, down_high[...], down_low[...])


def residual_mlp(rows, up, down):
    count, width = rows.shape
    middle = up.shape[1]
    block = math.gcd(count, 512)
    return pl.pallas_call(
        mlp_kernel,
        grid=(count // block,),
        in_specs=[
            pl.BlockSpec((block, width), lambda i: (i, 0)),
            pl.BlockSpec((width, middle), lambda i: (0, 0)),
            pl.BlockSpec((middle, width), lambda i: (0, 0)),
        ],
        out_specs=pl.BlockSpec((block, width), lambda i: (i, 0)),
        out_shape=jax.ShapeDtypeStruct((count, width), jnp.float32),
        scratch_shapes=[
            pltpu.VMEM((width, middle), jnp.bfloat16),
            pltpu.VMEM((width, middle), jnp.bfloat16),
            pltpu.VMEM((middle, width), jnp.bfloat16),
            pltpu.VMEM((middle, width), jnp.bfloat16),
        ],
        compiler_params=pltpu.CompilerParams(vmem_limit_bytes=40 * 2**20),
        cost_estimate=pl.CostEstimate(
            flops=12 * count * width * middle,
            bytes_accessed=8 * count * width,
            transcendentals=count * middle,
        ),
    )(rows, up, down)


def degree_exchange(blocks):
    return lax.all_to_all(blocks, ("lat", "lon"), split_axis=0, concat_axis=2, tiled=True)


def channel_join(matrix):
    return lax.all_gather(matrix, "feat", axis=1, tiled=True)


def feed_forward(inputs, up_weight, down_weight):
    whole_up = channel_join(up_weight)
    hidden = jax.nn.gelu(
        jnp.dot(inputs, whole_up, precision=best_precision, preferred_element_type=jnp.float32),
        approximate=False,
    )
    return jnp.dot(
        hidden, down_weight, precision=best_precision, preferred_element_type=jnp.float32
    )


def shards(
    atmosphere,
    spectral_weight,
    mlp_in,
    mlp_out,
    ocean_state,
    depth_kernel,
    depth_bias,
    norm_gain,
    ocean_up,
    ocean_down,
    ocean_bias,
    layer_scale,
    flux_weight,
    regrid_rows,
    ocean_rows,
    land_mask,
):
    lat_rows, lon_cols, half_chan = atmosphere.shape
    lon_devices = lax.axis_size("lon")
    lat_devices = lax.axis_size("lat")
    lat_index = lax.axis_index("lat")
    lon_index = lax.axis_index("lon")
    band_rows = lat_rows // lon_devices
    places = lat_devices * lon_devices
    degree_rows = LMAX // lat_devices
    mix_rows = degree_rows // lon_devices
    few_orders = MMAX // places
    flat_atm = atmosphere.reshape(-1, half_chan)
    picked = jnp.take(flat_atm, regrid_rows.reshape(-1), axis=0).reshape(lon_devices, -1, half_chan)
    arrived = lax.all_to_all(picked, "lon", split_axis=0, concat_axis=0, tiled=True)
    grid = regroup(atmosphere.reshape(lon_devices, band_rows, lon_cols, half_chan))
    spectrum = jnp.einsum(
        "anc,rnm->mrac", grid, forward_table(NLON, MMAX), precision=best_precision
    )
    spectrum = spectrum.reshape(places, few_orders, 2, band_rows, half_chan)
    row_ids = (lat_index * lon_devices + lon_index) * band_rows + jnp.arange(
        band_rows, dtype=jnp.int32
    )
    spectrum = spectrum * quadrature(row_ids, NLAT)[:, None]
    spread = lax.all_to_all(
        spectrum, ("lat", "lon"), split_axis=0, concat_axis=3, tiled=True
    )[0]
    orders = (lat_index * lon_devices + lon_index) * few_orders + jnp.arange(
        few_orders, dtype=jnp.int32
    )
    table = legendre_table(orders, LMAX, NLAT, MMAX)
    coeffs = jnp.einsum(
        "lmj,mrjc->lrmc", table, spread, precision=best_precision
    )
    mix_flat = degree_exchange(coeffs).reshape(-1, half_chan)
    mix_input = channel_join(mix_flat).reshape(mix_rows, 2, MMAX, C)
    real_part = jnp.einsum(
        "lmc,lcd->mld", mix_input[:, 0], spectral_weight[0], precision=best_precision
    ) - jnp.einsum("lmc,lcd->mld", mix_input[:, 1], spectral_weight[1], precision=best_precision)
    imag_part = jnp.einsum(
        "lmc,lcd->mld", mix_input[:, 1], spectral_weight[0], precision=best_precision
    ) + jnp.einsum("lmc,lcd->mld", mix_input[:, 0], spectral_weight[1], precision=best_precision)
    mixed = jnp.stack([real_part, imag_part], axis=1)
    back = degree_exchange(mixed)
    full_modes = jnp.einsum("lmj,mrlc->jrmc", table, back, precision=best_precision)
    wave_rows = lax.all_to_all(
        full_modes, ("lat", "lon"), split_axis=0, concat_axis=2, tiled=True
    )
    inverse = inverse_table(NLON, MMAX)
    whole_in = channel_join(mlp_in)
    whole_out = channel_join(mlp_out)
    pieces = 3 if band_rows % 6 == 0 else 1
    piece_rows = band_rows // pieces
    row_axis = 0 if piece_rows % 2 == 0 else 1
    finished = []
    for piece in range(pieces):
        span = slice(piece * piece_rows, (piece + 1) * piece_rows)
        summed = grid[span] + jnp.einsum(
            "armc,rmn->anc", wave_rows[span], inverse, precision=best_precision
        )
        full_input = lax.all_to_all(
            summed, "feat", split_axis=row_axis, concat_axis=2, tiled=True
        )
        result = residual_mlp(full_input.reshape(-1, C), whole_in, whole_out)
        result = lax.all_to_all(
            result.reshape(full_input.shape), "feat", split_axis=2, concat_axis=row_axis, tiled=True
        )
        result = result.reshape(piece_rows, lon_devices, lon_cols, half_chan)
        finished.append(
            lax.all_to_all(
                jnp.transpose(result, (1, 0, 2, 3)),
                "lon",
                split_axis=0,
                concat_axis=0,
                tiled=True,
            )
        )
    atmos_next = jnp.concatenate(finished, axis=1).reshape(lat_rows, lon_cols, half_chan)
    tile_rows, tile_cols, ocean_half = ocean_state.shape
    padded = with_halo(ocean_state, (("lat", 0), ("lon", 1)), KERNEL // 2)
    conv = jnp.zeros((tile_rows, tile_cols, ocean_half), jnp.float32) + depth_bias
    for tap_row in range(KERNEL):
        for tap_col in range(KERNEL):
            conv = (
                conv
                + padded[tap_row : tap_row + tile_rows, tap_col : tap_col + tile_cols]
                * depth_kernel[tap_row, tap_col]
            )
    arrived_full = channel_join(arrived.reshape(-1, half_chan))
    flux_rows = jnp.dot(
        arrived_full, flux_weight, precision=best_precision, preferred_element_type=jnp.float32
    )
    forcing = jnp.take(flux_rows, ocean_rows.reshape(-1), axis=0).reshape(
        tile_rows, tile_cols, ocean_half
    )
    joined = conv + forcing
    full_rows = channel_join(joined.reshape(-1, ocean_half))
    row_mean = jnp.mean(full_rows, axis=-1, keepdims=True)
    centered = full_rows - row_mean
    variance = jnp.mean(centered * centered, axis=-1, keepdims=True)
    normed = centered * lax.rsqrt(variance + 1e-06) * norm_gain
    update = feed_forward(normed, ocean_up, ocean_down) + ocean_bias
    mask_rows = tile_rows // BLOCK
    mask_cols = tile_cols // BLOCK
    cell_mask = (
        jnp.broadcast_to(land_mask[:, None, :, None], (mask_rows, BLOCK, mask_cols, BLOCK))
        .reshape(tile_rows, tile_cols)
        .astype(jnp.float32)
    )
    ocean_next = ocean_state + cell_mask[:, :, None] * layer_scale * update.reshape(
        tile_rows, tile_cols, ocean_half
    )
    return (atmos_next, ocean_next)


def solution(mesh):
    in_specs = (
        P("lat", "lon", "feat"),
        P(None, ("lat", "lon"), None, "feat"),
        P(None, "feat"),
        P(None, "feat"),
        P("lat", "lon", "feat"),
        P(None, None, "feat"),
        P("feat"),
        P(),
        P(None, "feat"),
        P(None, "feat"),
        P("feat"),
        P("feat"),
        P(None, "feat"),
        P("lat", "lon", None, None),
        P("lat", "lon"),
        P("lat", "lon"),
    )
    out_specs = (P("lat", "lon", "feat"), P("lat", "lon", "feat"))
    return jax.shard_map(shards, mesh=mesh, in_specs=in_specs, out_specs=out_specs, check_vma=False)
```

```python
import math

import jax
import jax.numpy as jnp
from jax import lax
from jax.experimental import pallas as pl
from jax.experimental.pallas import tpu as pltpu
from jax.sharding import PartitionSpec as P

C = 256
NLAT = 384
NLON = 768
LMAX = 384
MMAX = 256
KERNEL = 7
BLOCK = 8


best_precision = lax.Precision.HIGH


def with_halo(block, sides, width):
    for axis, dim in sides:
        count = lax.axis_size(axis)
        forward = [(i, i + 1) for i in range(count - 1)]
        backward = [(target, source) for source, target in forward]
        low = lax.ppermute(
            lax.slice_in_dim(block, block.shape[dim] - width, None, axis=dim), axis, forward
        )
        high = lax.ppermute(lax.slice_in_dim(block, 0, width, axis=dim), axis, backward)
        block = jnp.concatenate([low, block, high], axis=dim)
    return block


def legendre_table(orders, degree_count, lat_count, order_limit):
    index_lat = jnp.arange(lat_count, dtype=jnp.int32).astype(jnp.float32)
    colat = math.pi * (index_lat + 0.5) / lat_count
    cosine = jnp.cos(colat)
    sine = jnp.sin(colat)
    order_f = orders.astype(jnp.float32)[:, None]
    steps_k = jnp.arange(1, order_limit + 1, dtype=jnp.int32)
    step_f = steps_k.astype(jnp.float32)
    log_terms = jnp.log((2.0 * step_f + 1.0) / (2.0 * step_f))
    log_norm = jnp.sum(
        jnp.where(steps_k[None, :] <= orders[:, None], log_terms[None, :], 0.0), axis=1
    )
    log_start = 0.5 * (math.log(0.5) + log_norm[:, None]) + order_f * jnp.log(sine)[None, :]
    degree_f = jnp.arange(degree_count, dtype=jnp.int32).astype(jnp.float32)[:, None, None]
    order_sq = order_f * order_f
    factor_a = jnp.sqrt(
        jnp.maximum(4.0 * degree_f * degree_f - 1.0, 0.0)
        / jnp.maximum(degree_f * degree_f - order_sq, 1.0)
    )
    below = degree_f - 1.0
    factor_b = jnp.sqrt(
        jnp.maximum(below * below - order_sq, 0.0) / jnp.maximum(4.0 * below * below - 1.0, 1.0)
    )
    count = orders.shape[0]
    order_grid = jnp.broadcast_to(orders[:, None], (count, lat_count))
    chunk = math.gcd(degree_count, 48)

    def recur(start_ref, order_ref, cosine_ref, a_ref, b_ref, table_ref, state):
        @pl.when(pl.program_id(0) == 0)
        def _():
            state[...] = jnp.zeros_like(state)

        log_scale = start_ref[...]
        order = order_ref[...]
        cos_grid = cosine_ref[...]
        first = pl.program_id(0) * chunk
        current, previous, shift = state[0], state[1], state[2]
        for step in range(chunk):
            degree = first + step
            recurred = a_ref[step] * (cos_grid * current - b_ref[step] * previous)
            fresh = jnp.where(
                degree == order, 1.0, jnp.where(degree > order, recurred, 0.0)
            )
            large = jnp.abs(fresh) > 2.0**32
            rescale = jnp.where(large, 2.0 ** (-32), 1.0)
            fresh = fresh * rescale
            shift = shift + jnp.where(large, 32.0, 0.0)
            table_ref[step] = fresh * jnp.exp(log_scale + shift * math.log(2.0))
            current, previous = fresh, current * rescale
        state[0], state[1], state[2] = current, previous, shift

    whole = pl.BlockSpec((count, lat_count), lambda i: (0, 0))
    factor = pl.BlockSpec((chunk, count, 1), lambda i: (i, 0, 0))
    return pl.pallas_call(
        recur,
        grid=(degree_count // chunk,),
        in_specs=[whole, whole, whole, factor, factor],
        out_specs=pl.BlockSpec((chunk, count, lat_count), lambda i: (i, 0, 0)),
        out_shape=jax.ShapeDtypeStruct((degree_count, count, lat_count), jnp.float32),
        scratch_shapes=[pltpu.VMEM((3, count, lat_count), jnp.float32)],
        compiler_params=pltpu.CompilerParams(vmem_limit_bytes=32 * 2**20),
        cost_estimate=pl.CostEstimate(
            flops=60 * degree_count * count * lat_count,
            bytes_accessed=60 * degree_count * count * lat_count,
            transcendentals=degree_count * count * lat_count,
        ),
    )(
        log_start,
        order_grid,
        jnp.broadcast_to(cosine[None, :], (count, lat_count)),
        factor_a,
        factor_b,
    )


def quadrature(lat_ids, lat_count):
    colat = math.pi * (lat_ids.astype(jnp.float32) + 0.5) / lat_count
    return jnp.sin(colat) * (math.pi / lat_count)


def forward_table(lon_count, order_count):
    lon_ids = jnp.arange(lon_count, dtype=jnp.int32)[:, None]
    order_ids = jnp.arange(order_count, dtype=jnp.int32)[None, :]
    phase = 2.0 * math.pi / lon_count * (lon_ids * order_ids % lon_count).astype(jnp.float32)
    return jnp.stack([jnp.cos(phase), -jnp.sin(phase)], axis=0) / lon_count


def inverse_table(lon_count, order_count):
    order_ids = jnp.arange(order_count, dtype=jnp.int32)[:, None]
    lon_ids = jnp.arange(lon_count, dtype=jnp.int32)[None, :]
    phase = 2.0 * math.pi / lon_count * (order_ids * lon_ids % lon_count).astype(jnp.float32)
    weight = jnp.where(order_ids == 0, 1.0, 2.0)
    return jnp.stack([jnp.cos(phase) * weight, -jnp.sin(phase) * weight], axis=0)


def regroup(blocks):
    return lax.all_to_all(blocks, "lon", split_axis=0, concat_axis=2, tiled=True)[0]


def split_value(value):
    high = value.astype(jnp.bfloat16)
    return high, (value - high.astype(jnp.float32)).astype(jnp.bfloat16)


def split_dot(left, right_high, right_low):
    left_high, left_low = split_value(left)

    def part(one, other):
        return jnp.dot(one, other, preferred_element_type=jnp.float32)

    return part(left_high, right_high) + (
        part(left_high, right_low) + part(left_low, right_high)
    )


def mlp_kernel(rows_ref, up_ref, down_ref, out_ref, up_high, up_low, down_high, down_low):
    @pl.when(pl.program_id(0) == 0)
    def _():
        up_high[...], up_low[...] = split_value(up_ref[...])
        down_high[...], down_low[...] = split_value(down_ref[...])

    rows = rows_ref[...]
    pre = split_dot(rows, up_high[...], up_low[...])
    hidden = 0.5 * pre * (1.0 + lax.erf(pre * math.sqrt(0.5)))
    out_ref[...] = rows + split_dot(hidden, down_high[...], down_low[...])


def residual_mlp(rows, up, down):
    count, width = rows.shape
    middle = up.shape[1]
    block = math.gcd(count, 512)
    return pl.pallas_call(
        mlp_kernel,
        grid=(count // block,),
        in_specs=[
            pl.BlockSpec((block, width), lambda i: (i, 0)),
            pl.BlockSpec((width, middle), lambda i: (0, 0)),
            pl.BlockSpec((middle, width), lambda i: (0, 0)),
        ],
        out_specs=pl.BlockSpec((block, width), lambda i: (i, 0)),
        out_shape=jax.ShapeDtypeStruct((count, width), jnp.float32),
        scratch_shapes=[
            pltpu.VMEM((width, middle), jnp.bfloat16),
            pltpu.VMEM((width, middle), jnp.bfloat16),
            pltpu.VMEM((middle, width), jnp.bfloat16),
            pltpu.VMEM((middle, width), jnp.bfloat16),
        ],
        compiler_params=pltpu.CompilerParams(vmem_limit_bytes=40 * 2**20),
        cost_estimate=pl.CostEstimate(
            flops=12 * count * width * middle,
            bytes_accessed=8 * count * width,
            transcendentals=count * middle,
        ),
    )(rows, up, down)


def degree_exchange(blocks):
    return lax.all_to_all(blocks, ("lat", "lon"), split_axis=0, concat_axis=2, tiled=True)


def channel_join(matrix):
    return lax.all_gather(matrix, "feat", axis=1, tiled=True)


def feed_forward(inputs, up_weight, down_weight):
    whole_up = channel_join(up_weight)
    hidden = jax.nn.gelu(
        jnp.dot(inputs, whole_up, precision=best_precision, preferred_element_type=jnp.float32),
        approximate=False,
    )
    return jnp.dot(
        hidden, down_weight, precision=best_precision, preferred_element_type=jnp.float32
    )


def shards(
    atmosphere,
    spectral_weight,
    mlp_in,
    mlp_out,
    ocean_state,
    depth_kernel,
    depth_bias,
    norm_gain,
    ocean_up,
    ocean_down,
    ocean_bias,
    layer_scale,
    flux_weight,
    regrid_rows,
    ocean_rows,
    land_mask,
):
    lat_rows, lon_cols, half_chan = atmosphere.shape
    lon_devices = lax.axis_size("lon")
    lat_devices = lax.axis_size("lat")
    lat_index = lax.axis_index("lat")
    lon_index = lax.axis_index("lon")
    band_rows = lat_rows // lon_devices
    places = lat_devices * lon_devices
    degree_rows = LMAX // lat_devices
    mix_rows = degree_rows // lon_devices
    few_orders = MMAX // places
    flat_atm = atmosphere.reshape(-1, half_chan)
    picked = jnp.take(flat_atm, regrid_rows.reshape(-1), axis=0).reshape(lon_devices, -1, half_chan)
    arrived = lax.all_to_all(picked, "lon", split_axis=0, concat_axis=0, tiled=True)
    grid = regroup(atmosphere.reshape(lon_devices, band_rows, lon_cols, half_chan))
    padded = with_halo(ocean_state, (("lat", 0), ("lon", 1)), KERNEL // 2)
    grid, padded, arrived = lax.optimization_barrier((grid, padded, arrived))
    spectrum = jnp.einsum(
        "anc,rnm->mrac", grid, forward_table(NLON, MMAX), precision=best_precision
    )
    spectrum = spectrum.reshape(places, few_orders, 2, band_rows, half_chan)
    row_ids = (lat_index * lon_devices + lon_index) * band_rows + jnp.arange(
        band_rows, dtype=jnp.int32
    )
    spectrum = spectrum * quadrature(row_ids, NLAT)[:, None]
    spread = lax.all_to_all(
        spectrum, ("lat", "lon"), split_axis=0, concat_axis=3, tiled=True
    )[0]
    orders = (lat_index * lon_devices + lon_index) * few_orders + jnp.arange(
        few_orders, dtype=jnp.int32
    )
    table = legendre_table(orders, LMAX, NLAT, MMAX)
    coeffs = jnp.einsum(
        "lmj,mrjc->lrmc", table, spread, precision=best_precision
    )
    mix_flat = degree_exchange(coeffs).reshape(-1, half_chan)
    mix_input = channel_join(mix_flat).reshape(mix_rows, 2, MMAX, C)
    real_part = jnp.einsum(
        "lmc,lcd->mld", mix_input[:, 0], spectral_weight[0], precision=best_precision
    ) - jnp.einsum("lmc,lcd->mld", mix_input[:, 1], spectral_weight[1], precision=best_precision)
    imag_part = jnp.einsum(
        "lmc,lcd->mld", mix_input[:, 1], spectral_weight[0], precision=best_precision
    ) + jnp.einsum("lmc,lcd->mld", mix_input[:, 0], spectral_weight[1], precision=best_precision)
    mixed = jnp.stack([real_part, imag_part], axis=1)
    back = degree_exchange(mixed)
    full_modes = jnp.einsum("lmj,mrlc->jrmc", table, back, precision=best_precision)
    wave_rows = lax.all_to_all(
        full_modes, ("lat", "lon"), split_axis=0, concat_axis=2, tiled=True
    )
    tile_rows, tile_cols, ocean_half = ocean_state.shape
    conv = jnp.zeros((tile_rows, tile_cols, ocean_half), jnp.float32) + depth_bias
    for tap_row in range(KERNEL):
        for tap_col in range(KERNEL):
            conv = (
                conv
                + padded[tap_row : tap_row + tile_rows, tap_col : tap_col + tile_cols]
                * depth_kernel[tap_row, tap_col]
            )
    arrived_full = channel_join(arrived.reshape(-1, half_chan))
    flux_rows = jnp.dot(
        arrived_full, flux_weight, precision=best_precision, preferred_element_type=jnp.float32
    )
    forcing = jnp.take(flux_rows, ocean_rows.reshape(-1), axis=0).reshape(
        tile_rows, tile_cols, ocean_half
    )
    joined = conv + forcing
    full_rows = channel_join(joined.reshape(-1, ocean_half))
    row_mean = jnp.mean(full_rows, axis=-1, keepdims=True)
    centered = full_rows - row_mean
    variance = jnp.mean(centered * centered, axis=-1, keepdims=True)
    normed = centered * lax.rsqrt(variance + 1e-06) * norm_gain
    update = feed_forward(normed, ocean_up, ocean_down) + ocean_bias
    mask_rows = tile_rows // BLOCK
    mask_cols = tile_cols // BLOCK
    cell_mask = (
        jnp.broadcast_to(land_mask[:, None, :, None], (mask_rows, BLOCK, mask_cols, BLOCK))
        .reshape(tile_rows, tile_cols)
        .astype(jnp.float32)
    )
    ocean_next = ocean_state + cell_mask[:, :, None] * layer_scale * update.reshape(
        tile_rows, tile_cols, ocean_half
    )
    wave_rows, ocean_next = lax.optimization_barrier((wave_rows, ocean_next))
    inverse = inverse_table(NLON, MMAX)
    whole_in = channel_join(mlp_in)
    whole_out = channel_join(mlp_out)
    pieces = 3 if band_rows % 6 == 0 else 1
    piece_rows = band_rows // pieces
    row_axis = 0 if piece_rows % 2 == 0 else 1
    finished = []
    for piece in range(pieces):
        span = slice(piece * piece_rows, (piece + 1) * piece_rows)
        summed = grid[span] + jnp.einsum(
            "armc,rmn->anc", wave_rows[span], inverse, precision=best_precision
        )
        full_input = lax.all_to_all(
            summed, "feat", split_axis=row_axis, concat_axis=2, tiled=True
        )
        result = residual_mlp(full_input.reshape(-1, C), whole_in, whole_out)
        result = lax.all_to_all(
            result.reshape(full_input.shape), "feat", split_axis=2, concat_axis=row_axis, tiled=True
        )
        result = result.reshape(piece_rows, lon_devices, lon_cols, half_chan)
        finished.append(
            lax.all_to_all(
                jnp.transpose(result, (1, 0, 2, 3)),
                "lon",
                split_axis=0,
                concat_axis=0,
                tiled=True,
            )
        )
    atmos_next = jnp.concatenate(finished, axis=1).reshape(lat_rows, lon_cols, half_chan)
    return (atmos_next, ocean_next)


def solution(mesh):
    in_specs = (
        P("lat", "lon", "feat"),
        P(None, ("lat", "lon"), None, "feat"),
        P(None, "feat"),
        P(None, "feat"),
        P("lat", "lon", "feat"),
        P(None, None, "feat"),
        P("feat"),
        P(),
        P(None, "feat"),
        P(None, "feat"),
        P("feat"),
        P("feat"),
        P(None, "feat"),
        P("lat", "lon", None, None),
        P("lat", "lon"),
        P("lat", "lon"),
    )
    out_specs = (P("lat", "lon", "feat"), P("lat", "lon", "feat"))
    return jax.shard_map(shards, mesh=mesh, in_specs=in_specs, out_specs=out_specs, check_vma=False)
```
